256 devices in a mesh: replica: 8 (over x, core), fsdp: 16 (over y_lo, z), tensor: 2 (over y_hi).
Axes of the slice: x: 4, y: 4 (y_hi: 2, y_lo: 2; y = y_hi * 2 + y_lo), z: 8, core: 2. Of those that a mesh axis runs over, the one named last changes fastest.
Arguments:
- pseudo_grads: float32 [8, 4096, 5120], P('replica', 'fsdp', 'tensor'), may hold values from -6 to 6
- counts: int32 [8], P('replica'), may hold values from 1024 to 8703, as said below
- master: float32 [4096, 5120], P(('fsdp', 'replica'), 'tensor')
- momentum: float32 [4096, 5120], P(('fsdp', 'replica'), 'tensor'), may hold values from -4 to 4
- tokens: bfloat16 [128, 512, 4096], P(('replica', 'fsdp'), None, 'tensor')
- norm_gain: float32 [4096], replicated, may hold values from 0.1 to 1.9
- lengths: int32 [128], P(('replica', 'fsdp')), may hold values from 128 to 512, as said below
Outputs:
- new_master: float32 [4096, 5120], P(('fsdp', 'replica'), 'tensor')
- new_momentum: float32 [4096, 5120], P(('fsdp', 'replica'), 'tensor')
- context: bfloat16 [128, 512, 4096], P(('replica', 'fsdp'), None, 'tensor')
The draws below stay inside these ranges and needn't reach their ends.
Inputs may be any that keep to these rules, and one draw needn't show every extreme that they name: `lengths`: live positions of each batch row; later positions are padding, and some row is full. `counts`: tokens each replica processed; both ends of the range are reached.
All inputs are finite; a program needn't handle non-finite values.
Results may differ from the reference program's by a relative error of at most 0.0089.
The reference program's roundings to bfloat16 on the way (of `weights`, `normed` and `probs`) count: a program that leaves them out, or rounds other values in their place, can miss the bound.
Values may be sent and summed in bfloat16 or wider, within the bound.
No kernel may reach another device: no remote copies, remote signals or barrier semaphores. Data moves between devices by JAX's collectives and lax.ppermute only.
A program may use at most 128 MiB of HBM per device.

```python
import jax
import jax.numpy as jnp
from jax import lax

D = 4096
HD = 128
QPK = 8
SEQ = 512
COLS = 5120
BATCH = 128
N_REPLICA = 8


def draw_counts(key, part):
    key = jax.random.fold_in(key, 14)
    extra = jax.random.randint(key, (N_REPLICA,), 0, 512, jnp.int32)
    index = jnp.arange(N_REPLICA, dtype=jnp.int32)
    extra = jnp.where(index == 0, 0, extra)
    extra = jnp.where(index == N_REPLICA - 1, 511, extra)
    rising = (index + 1) * 1024
    return (rising + extra).astype(jnp.int32)


def draw_master(key, part):
    key = jax.random.fold_in(key, 11)
    return jax.random.normal(key, (D, COLS), jnp.float32)


def draw_tokens(key, part):
    key = jax.random.fold_in(key, 12)
    first = jax.random.fold_in(key, 0)
    return jax.random.normal(first, (BATCH, SEQ, D), jnp.float32).astype(jnp.bfloat16)


def draw_lengths(key, part):
    key = jax.random.fold_in(key, 13)
    first, second = jax.random.split(key)
    drawn = jax.random.randint(first, (BATCH,), SEQ // 4, SEQ + 1, jnp.int32)
    chosen = jax.random.randint(second, (), 0, BATCH, jnp.int32)
    return jnp.where(jnp.arange(BATCH, dtype=jnp.int32) == chosen, SEQ, drawn).astype(jnp.int32)


def strengthened(entries, stream_key, source, target, shards_of, factor):
    owner, partner = [(jnp.arange(entries.shape[dim]) // (entries.shape[dim] // shards_of)).reshape([-1 if axis == dim else 1 for axis in range(entries.ndim)]) for dim in (source, target)]
    chosen = jax.random.permutation(stream_key, shards_of)[partner]
    strong = (owner == chosen) | (owner == (partner + shards_of // 2) % shards_of)
    return jnp.where(strong, factor * entries, entries)


def block_levels(key, shape, cuts, least, high):
    level = 1.0
    for dim, blocks in cuts:
        steps = jax.random.uniform(jax.random.fold_in(jax.random.fold_in(key, 6), dim), (blocks,), jnp.float32, least / len(cuts), high / len(cuts))
        level = level * jnp.repeat(jnp.exp(steps), shape[dim] // blocks).reshape((-1,) + (1,) * (len(shape) - 1 - dim))
    return level


def noise(key, shape, spread, reach, cuts=(), kind=jnp.bfloat16):
    factor_of = block_levels(key, shape, cuts, -0.22, 0.18) if cuts else 1.0
    entries = jax.random.normal(key, shape, jnp.float32) * spread * factor_of
    return jnp.minimum(jnp.maximum(entries, -reach), reach).astype(kind)


def bell_draw_with(own_key, shape, deviation, reach, cuts, heavy, held_as=jnp.bfloat16):
    result = deviation * jax.random.normal(own_key, shape, jnp.float32)
    if cuts:
        result = result * block_levels(own_key, shape, cuts, -0.22, 0.18)
    return jnp.clip(strengthened(result, jax.random.fold_in(own_key, 3), *heavy), -reach, reach).astype(held_as)


def setup_inputs(seed: int = 0) -> dict:
    splits = jax.random.split(jax.random.key(seed), 8)
    pseudo_grads = bell_draw_with(splits[0], (N_REPLICA, D, COLS), 1.0, 6.0, ((0, 8), (1, 16), (2, 2)), (0, 1, 8, 2.0), jnp.float32)
    counts = draw_counts(jax.random.fold_in(splits[7], 71), 0)
    master = draw_master(jax.random.fold_in(splits[7], 71), 0)
    momentum = noise(splits[3], (D, COLS), 0.5, 4.0, ((0, 128), (1, 2)), jnp.float32)
    tokens = draw_tokens(jax.random.fold_in(splits[7], 71), 0)
    norm_gain = jnp.clip(1.0 + 0.18 * jax.random.normal(splits[5], (D,), jnp.float32), 0.1, 1.9)
    lengths = draw_lengths(jax.random.fold_in(splits[7], 71), 0)
    return dict(pseudo_grads=pseudo_grads, counts=counts, master=master, momentum=momentum, tokens=tokens, norm_gain=norm_gain, lengths=lengths)


outer_momentum = 0.9
outer_rate = 0.7

def normalize(rows, gain):
    values = rows.astype(jnp.float32)
    scale = lax.rsqrt(lax.optimization_barrier(jnp.mean(values * values, axis=-1, keepdims=True)) + 1e-05)
    return (values * scale * gain).astype(jnp.bfloat16)

def rotate(values):
    length = values.shape[1]
    half = HD // 2
    freq = 500000.0 ** (-(jnp.arange(half, dtype=jnp.float32) * 2.0 / HD))
    angle = jnp.arange(length, dtype=jnp.float32)[:, None] * freq[None, :]
    shape = (1, length) + (1,) * (values.ndim - 3) + (half,)
    cosine = jnp.cos(angle).reshape(shape)
    sine = jnp.sin(angle).reshape(shape)
    first = values[..., :half]
    second = values[..., half:]
    return jnp.concatenate([first * cosine - second * sine, second * cosine + first * sine], axis=-1)

def attention(proj, lens):
    batch, length, width = proj.shape
    groups = width // ((QPK + 2) * HD)
    parts = proj.reshape(batch, length, groups, QPK + 2, HD)
    query = rotate(parts[:, :, :, :QPK]).astype(jnp.bfloat16)
    keys = rotate(parts[:, :, :, QPK]).astype(jnp.bfloat16)
    values = parts[:, :, :, QPK + 1].astype(jnp.bfloat16)
    scores = jnp.einsum('rsgqh,rtgh->rgqst', query.astype(jnp.float32), keys.astype(jnp.float32)) * HD ** (-0.5)
    position = jnp.arange(length, dtype=jnp.int32)
    causal = (position[None, :] <= position[:, None])[None, None, None]
    inside = position[None, None, None, None, :] < lens.reshape(batch, 1, 1, 1, 1)
    scores = jnp.where(causal & inside, scores, -1e+30)
    top = lax.optimization_barrier(jnp.max(scores, axis=-1, keepdims=True))
    raised = jnp.exp(scores - top)
    probs = (raised / lax.optimization_barrier(jnp.sum(raised, axis=-1, keepdims=True))).astype(jnp.bfloat16)
    mixed = jnp.einsum('rgqst,rtgh->rsgqh', probs.astype(jnp.float32), values.astype(jnp.float32))
    live = (position[None, :] < lens[:, None]).reshape(batch, length, 1, 1, 1)
    return jnp.where(live, mixed, 0.0).astype(jnp.bfloat16).reshape(batch, length, groups * QPK * HD)

def reference(pseudo_grads, counts, master, momentum, tokens, norm_gain, lengths):
    count_f = counts.astype(jnp.float32)
    total = jnp.sum(count_f)

    def accumulate(carry, packed):
        grads, weight = packed
        return (carry + weight * grads, None)
    summed, _ = lax.scan(accumulate, jnp.zeros(master.shape, jnp.float32), (pseudo_grads, count_f))
    delta = summed / total
    new_momentum = outer_momentum * momentum + delta
    new_master = master - outer_rate * (delta + outer_momentum * new_momentum)
    weights = new_master.astype(jnp.bfloat16)

    def one_row(packed):
        row, length = packed
        normed = normalize(row[None], norm_gain)
        proj = jnp.dot(normed.reshape(SEQ, D), weights, preferred_element_type=jnp.float32) * D ** (-0.5)
        return attention(proj.reshape(1, SEQ, COLS), length.reshape(1))[0]
    context = lax.map(one_row, (tokens, lengths))
    return (new_master, new_momentum, context)
```

```python
import functools

import jax
import jax.numpy as jnp
from jax import lax
from jax.experimental import pallas as pl
from jax.experimental.pallas import tpu as pltpu
from jax.sharding import PartitionSpec as P

D = 4096
HD = 128
QPK = 8
SEQ = 512
GROUP = (QPK + 2) * HD
HALF = D // 2
VMEM_LIMIT = 60 << 20
LOG2E = 1.4426950408889634
AXES = ("replica", "fsdp", "tensor")
NX, NC, NY, NZ = 4, 2, 2, 8

outer_momentum = 0.9
outer_rate = 0.7


def device(x, c, y, z, h):
    return (((x % NX) * NC + c) * NY * NZ + y * NZ + z % NZ) * 2 + h


def places():
    for x in range(NX):
        for c in range(NC):
            for y in range(NY):
                for z in range(NZ):
                    for h in range(2):
                        yield x, c, y, z, h


def pairs(target):
    return [(device(*p), device(*target(*p))) for p in places()]


def send(value, target):
    return lax.ppermute(value, AXES, pairs(target))


def after(value, *others):
    return lax.optimization_barrier((value, *others))[0]


def sibling(x, c, y, z, h):
    return x, 1 - c, y, z, h


def partner(x, c, y, z, h):
    return x, c, y, z, 1 - h


def along_x(step):
    return lambda x, c, y, z, h: (x + step, c, y, z, h)


NEAR = ((2, 0), (1, 0), (3, 0), (2, 1), (1, 1), (3, 1), (0, 1))
NEAR_Z = (4, 3, -3, 2, -2, 1, -1)


def near_target(i):
    def target(x, c, y, z, h):
        if c == 0:
            return x + NEAR[i][0], c, (y + NEAR[i][1]) % NY, z, h
        return x, c, y, z + NEAR_Z[i], h

    return target


def near_gather(own):
    first = [send(own, near_target(i)) for i in range(3)]
    own_later = after(own, *first)
    return [own] + first + [send(own_later, near_target(i)) for i in range(3, 7)]


def far_groups():
    groups = []
    for h in range(2):
        for x in range(NX):
            for y in range(NY):
                groups.append([device(x, 0, y, z, h) for z in range(NZ)])
        for z in range(NZ):
            groups.append([device(x, 1, y, z, h) for y in range(NY) for x in range(NX)])
    return groups


def place_kernel(at_ref, *refs):
    *blocks, out = refs
    for i, block in enumerate(blocks):
        rows = block.shape[0]
        start = pl.multiple_of(at_ref[i], 64)
        out[pl.ds(start, rows), :] = block[...]


def place(at, blocks):
    width = blocks[0].shape[1]
    total = sum(b.shape[0] for b in blocks)
    return pl.pallas_call(
        place_kernel,
        out_shape=jax.ShapeDtypeStruct((total, width), blocks[0].dtype),
        grid_spec=pltpu.PrefetchScalarGridSpec(
            num_scalar_prefetch=1,
            grid=(1,),
            in_specs=[pl.BlockSpec(b.shape, lambda i, at: (0, 0)) for b in blocks],
            out_specs=pl.BlockSpec((total, width), lambda i, at: (0, 0)),
        ),
        compiler_params=pltpu.CompilerParams(vmem_limit_bytes=VMEM_LIMIT),
        cost_estimate=pl.CostEstimate(
            flops=0, transcendentals=0, bytes_accessed=4 * total * width
        ),
        name="place",
    )(at, *blocks)


def norm_kernel(high_ref, own, other, gain, out):
    first, second = own[...].astype(jnp.float32), other[...].astype(jnp.float32)
    square = jnp.sum(first * first + second * second, axis=-1, keepdims=True)
    scale = lax.rsqrt(square * (1.0 / D) + 1e-05)
    keep = high_ref[0] == 0
    for a, b, start in ((first, second, 0), (second, first, HALF)):
        values = jnp.where(keep, a, b) * scale * gain[:, start : start + HALF]
        out[:, start : start + HALF] = values.astype(jnp.bfloat16)


def normalize(high, own, other, gain):
    tile = 64
    count = own.shape[0]
    rows = pl.BlockSpec((tile, HALF), lambda i, w: (i, 0))
    return pl.pallas_call(
        norm_kernel,
        out_shape=jax.ShapeDtypeStruct((count, D), jnp.bfloat16),
        grid_spec=pltpu.PrefetchScalarGridSpec(
            num_scalar_prefetch=1,
            grid=(count // tile,),
            in_specs=[rows, rows, pl.BlockSpec((1, D), lambda i, w: (0, 0))],
            out_specs=pl.BlockSpec((tile, D), lambda i, w: (i, 0)),
        ),
        compiler_params=pltpu.CompilerParams(vmem_limit_bytes=VMEM_LIMIT),
        cost_estimate=pl.CostEstimate(
            flops=8 * count * D, transcendentals=0, bytes_accessed=4 * count * D
        ),
        name="normalize",
    )(high, own, other, gain.reshape(1, D))


def project_kernel(
    core_ref, own_low, own_high, sib_low, sib_high, by_z, by_plane, out, rows
):
    for i, (low, high) in enumerate(((own_low, own_high), (sib_low, sib_high))):
        rows[i * SEQ : (i + 1) * SEQ, :512] = low[...]
        rows[i * SEQ : (i + 1) * SEQ, 512:] = high[...]

    def add(weights):
        part = jnp.dot(rows[...], weights, preferred_element_type=jnp.float32)
        part = part.reshape(out.shape)

        @pl.when(pl.program_id(0) == 0)
        def _():
            out[...] = part

        @pl.when(pl.program_id(0) > 0)
        def _():
            out[...] += part

    @pl.when(core_ref[0] == 0)
    def _():
        add(jnp.concatenate([by_z[i * 256 : (i + 1) * 256] for i in (0, 2, 1, 3)]))

    @pl.when(core_ref[0] == 1)
    def _():
        add(
            jnp.concatenate(
                [
                    by_plane[y, :, z].reshape(256, by_plane.shape[-1])
                    for y in range(NY)
                    for z in range(2)
                ]
            )
        )


def project(core, normed, weights):
    width = weights.shape[1]
    steps = NZ // 2
    low = pl.BlockSpec((SEQ, 512), lambda t, core: (0, t))
    high = pl.BlockSpec((SEQ, 512), lambda t, core: (0, steps + t))
    shape = (2, SEQ, width)
    own, sib = normed
    return pl.pallas_call(
        project_kernel,
        out_shape=jax.ShapeDtypeStruct(shape, jnp.float32),
        grid_spec=pltpu.PrefetchScalarGridSpec(
            num_scalar_prefetch=1,
            grid=(steps,),
            in_specs=[low, high, low, high]
            + [
                pl.BlockSpec((1024, width), lambda t, core: (jnp.where(core[0] == 0, t, 0), 0)),
                pl.BlockSpec(
                    (NY, NX, 2, 64, width),
                    lambda t, core: (0, 0, jnp.where(core[0] == 0, 0, t), 0, 0),
                ),
            ],
            out_specs=pl.BlockSpec(shape, lambda t, core: (0, 0, 0)),
            scratch_shapes=[pltpu.VMEM((2 * SEQ, 1024), jnp.bfloat16)],
        ),
        compiler_params=pltpu.CompilerParams(vmem_limit_bytes=VMEM_LIMIT),
        cost_estimate=pl.CostEstimate(
            flops=4 * SEQ * D * width,
            transcendentals=0,
            bytes_accessed=2 * D * width + 4 * SEQ * D + 8 * SEQ * width,
        ),
        name="project",
    )(core, own, own, sib, sib, weights, weights.reshape(NY, NX, NZ, 64, width))


def turn(values, cosine, sine):
    return values * cosine + pltpu.roll(values, HD // 2, 1) * sine


def attend_kernel(at_ref, q_ref, kv_ref, cos_ref, sin_ref, mine, theirs, key, value):
    row = pl.program_id(0)
    length = at_ref[row]
    cosine, sine = cos_ref[...], sin_ref[...]
    unit = D**-0.5
    tile = 256

    @pl.when(pl.program_id(1) == 0)
    def _():
        key[...] = turn(kv_ref[0, :, :HD] * unit, cosine, sine).astype(jnp.bfloat16)
        value[...] = (kv_ref[0, :, HD:] * unit).astype(jnp.bfloat16)

    s = lax.broadcasted_iota(jnp.int32, (tile, tile), 0)
    t = lax.broadcasted_iota(jnp.int32, (tile, tile), 1)
    heads = range(2)
    queries = [
        turn(q_ref[0, :, h * HD : (h + 1) * HD] * unit, cosine, sine).astype(jnp.bfloat16)
        for h in heads
    ]
    results = {}
    for block in range(SEQ // tile):
        start, reach = block * tile, (block + 1) * tile
        allowed = [jnp.where((t <= s) & (t + start < length), 0.0, -1e30)]
        if block:
            allowed.insert(0, jnp.where(t < length, 0.0, -1e30))
        live = lax.broadcasted_iota(jnp.int32, (tile, HD), 0) + start < length
        scores = lax.dot_general(
            jnp.concatenate([q[start:reach] for q in queries], axis=0),
            key[:reach],
            (((1,), (1,)), ((), ())),
            preferred_element_type=jnp.float32,
        )
        mask = jnp.concatenate(allowed, axis=1)
        scores = scores.reshape(len(heads), tile, reach) * (HD ** (-0.5) * LOG2E) + mask[None]
        scores = scores.reshape(len(heads) * tile, reach)
        raised = jnp.exp2(scores - jnp.max(scores, axis=1, keepdims=True))
        scale = 1.0 / jnp.sum(raised, axis=1, keepdims=True)
        mixed = jnp.dot(
            raised.astype(jnp.bfloat16), value[:reach], preferred_element_type=jnp.float32
        )
        mixed = mixed * scale
        for h in heads:
            results[start, h * HD] = jnp.where(
                live, mixed[h * tile : (h + 1) * tile], 0.0
            ).astype(jnp.bfloat16)

    def fill(out):
        for (start, column), part in results.items():
            out[start : start + tile, column : column + HD] = part

    pl.when(row == 0)(lambda: fill(mine))
    pl.when(row == 1)(lambda: fill(theirs))


def attend(lens, column, proj, cosine, sine):
    width = QPK * HD
    count = width // (2 * HD)
    at = jnp.concatenate([lens, jnp.reshape(column // (2 * HD), (1,))])
    return pl.pallas_call(
        attend_kernel,
        out_shape=(
            jax.ShapeDtypeStruct((SEQ, 2 * width), jnp.bfloat16),
            jax.ShapeDtypeStruct((SEQ, width), jnp.bfloat16),
        ),
        grid_spec=pltpu.PrefetchScalarGridSpec(
            num_scalar_prefetch=1,
            grid=(2, count),
            in_specs=[
                pl.BlockSpec((1, SEQ, 2 * HD), lambda r, j, at: (r, 0, j)),
                pl.BlockSpec((1, SEQ, 2 * HD), lambda r, j, at: (r, 0, count)),
                pl.BlockSpec((SEQ, HD), lambda r, j, at: (0, 0)),
                pl.BlockSpec((SEQ, HD), lambda r, j, at: (0, 0)),
            ],
            out_specs=(
                pl.BlockSpec(
                    (SEQ, 2 * HD), lambda r, j, at: (0, at[2] + jnp.where(r == 0, j, count - 1))
                ),
                pl.BlockSpec((SEQ, 2 * HD), lambda r, j, at: (0, jnp.where(r == 0, 0, j))),
            ),
            scratch_shapes=[
                pltpu.VMEM((SEQ, HD), jnp.bfloat16),
                pltpu.VMEM((SEQ, HD), jnp.bfloat16),
            ],
        ),
        compiler_params=pltpu.CompilerParams(vmem_limit_bytes=VMEM_LIMIT),
        cost_estimate=pl.CostEstimate(
            flops=8 * SEQ * SEQ * width,
            transcendentals=2 * SEQ * SEQ * width // HD,
            bytes_accessed=12 * SEQ * width,
        ),
        name="attend",
    )(at, proj, proj, cosine, sine)


def insert_kernel(at_ref, part, _, out):
    out[...] = part[...]


def insert(column, part, context):
    width = 2 * HD
    return pl.pallas_call(
        insert_kernel,
        out_shape=jax.ShapeDtypeStruct(context.shape, context.dtype),
        grid_spec=pltpu.PrefetchScalarGridSpec(
            num_scalar_prefetch=1,
            grid=(part.shape[1] // width,),
            in_specs=[
                pl.BlockSpec((SEQ, width), lambda j, at: (0, j)),
                pl.BlockSpec(memory_space=pl.ANY),
            ],
            out_specs=pl.BlockSpec((SEQ, width), lambda j, at: (0, at[0] + j)),
        ),
        input_output_aliases={2: 0},
        compiler_params=pltpu.CompilerParams(vmem_limit_bytes=VMEM_LIMIT),
        cost_estimate=pl.CostEstimate(
            flops=0, transcendentals=0, bytes_accessed=4 * SEQ * part.shape[1]
        ),
        name="insert",
    )(jnp.reshape(column // width, (1,)), part, context)


def per_device(pseudo_grads, counts, master, momentum, tokens, norm_gain, lengths):
    replica, fsdp = lax.axis_index("replica"), lax.axis_index("fsdp")
    x, core = replica // NC, replica % NC
    y, z = fsdp // NZ, fsdp % NZ
    cycle = jnp.where(y == 0, x, 7 - x)

    weight = counts[0].astype(jnp.float32)

    half = HD // 2
    freq = 500000.0 ** (-(jnp.arange(half, dtype=jnp.float32) * 2.0 / HD))
    angle = jnp.arange(SEQ, dtype=jnp.float32)[:, None] * freq[None, :]
    cosine, sine = jnp.cos(angle), jnp.sin(angle)
    cosine = jnp.concatenate([cosine, cosine], axis=1)
    sine = jnp.concatenate([-sine, sine], axis=1)

    def mine(array):
        return lax.dynamic_slice_in_dim(array, core * GROUP, GROUP, axis=1)

    def theirs(array):
        return lax.dynamic_slice_in_dim(array, (1 - core) * GROUP, GROUP, axis=1)

    grads = pseudo_grads[0]
    own_tokens = tokens[0]
    other_tokens = send(own_tokens, partner)


    counted = jnp.broadcast_to(weight, (8, GROUP))
    got = send(jnp.concatenate([theirs(grads) * weight, counted]), sibling)
    states = send(
        after(
            jnp.concatenate(
                [
                    theirs(master),
                    theirs(momentum),
                    jnp.broadcast_to(lengths[0].astype(jnp.float32), (8, GROUP)),
                ]
            ),
            got,
        ),
        sibling,
    )
    lens = jnp.stack([lengths[0], states[64, 0].astype(jnp.int32)])

    places_at = [jnp.where(core == 0, y * NX + x, z)]
    for (dx, dy), dz in zip(NEAR, NEAR_Z):
        plane = (y + NY - dy) % NY * NX + (x + NX - dx) % NX
        places_at.append(jnp.where(core == 0, plane, (z + NZ - dz) % NZ))
    places_at = (jnp.stack(places_at) * 64).astype(jnp.int32)

    summed = mine(grads) * weight + got[:256]
    part = summed.reshape(NX, 64, GROUP)

    def block(step):
        value = lax.dynamic_index_in_dim(part, (x + step) % NX, 0, keepdims=False)
        return jnp.concatenate([value, counted + got[256:]])

    arrived = [send(block(step), along_x(step)) for step in (1, 3, 2)]
    summed = block(0) + arrived[0] + arrived[1] + arrived[2]
    delta = summed[:64] / summed[64, 0]
    pair = []
    for array, kept in ((master, states[:32]), (momentum, states[32:64])):
        a, b = mine(array), kept
        pair.append(
            jnp.concatenate([jnp.where(core == 0, a, b), jnp.where(core == 0, b, a)], axis=0)
        )
    new_momentum = outer_momentum * pair[1] + delta
    new_master = pair[0] - outer_rate * (delta + outer_momentum * new_momentum)
    near = near_gather(new_master.astype(jnp.bfloat16))
    near[0] = after(near[0], other_tokens)
    whole = place(places_at, near)

    def in_order(own, other):
        return jnp.concatenate(
            [jnp.where(core == 0, own, other), jnp.where(core == 0, other, own)], axis=1
        )

    both = (new_master, new_momentum)
    back = send(
        after(
            jnp.concatenate([jnp.where(core == 0, v[32:], v[:32]) for v in both], axis=0),
            whole,
        ),
        sibling,
    )
    outs = [
        in_order(jnp.where(core == 0, v[:32], v[32:]), back[32 * i : 32 * (i + 1)])
        for i, v in enumerate(both)
    ]

    core_id = jnp.reshape(core, (1,)).astype(jnp.int32)
    high_id = jnp.reshape(lax.axis_index("tensor"), (1,)).astype(jnp.int32)
    full = lax.all_gather(whole, AXES, axis=0, tiled=True, axis_index_groups=far_groups())
    kept = normalize(high_id, own_tokens, after(other_tokens, whole), norm_gain)
    normed = (kept, send(kept, sibling))

    full, *outs = lax.optimization_barrier((full, *outs))
    proj = project(core_id, normed, full)
    context, given = attend(lens, core * QPK * HD, proj, cosine, sine)
    context = insert((1 - core) * QPK * HD, send(given, sibling), context)
    return outs[0], outs[1], context[None]


def solution(mesh):
    in_specs = (
        P("replica", "fsdp", "tensor"),
        P("replica"),
        P(("fsdp", "replica"), "tensor"),
        P(("fsdp", "replica"), "tensor"),
        P(("replica", "fsdp"), None, "tensor"),
        P(),
        P(("replica", "fsdp")),
    )
    out_specs = (
        P(("fsdp", "replica"), "tensor"),
        P(("fsdp", "replica"), "tensor"),
        P(("replica", "fsdp"), None, "tensor"),
    )
    return jax.shard_map(
        per_device, mesh=mesh, in_specs=in_specs, out_specs=out_specs, check_vma=False
    )
```

```python
import jax
import jax.numpy as jnp
from jax import lax
from jax.experimental import pallas as pl
from jax.experimental.pallas import tpu as pltpu
from jax.sharding import PartitionSpec as P

D = 4096
HD = 128
QPK = 8
SEQ = 512
GROUP = (QPK + 2) * HD
HALF = D // 2
VMEM_LIMIT = 60 << 20
LOG2E = 1.4426950408889634
AXES = ("replica", "fsdp", "tensor")
NX, NC, NY, NZ = 4, 2, 2, 8

outer_momentum = 0.9
outer_rate = 0.7


def device(x, c, y, z, h):
    return (((x % NX) * NC + c) * NY * NZ + y * NZ + z % NZ) * 2 + h


def places():
    for x in range(NX):
        for c in range(NC):
            for y in range(NY):
                for z in range(NZ):
                    for h in range(2):
                        yield x, c, y, z, h


def pairs(target):
    return [(device(*p), device(*target(*p))) for p in places()]


def send(value, target):
    return lax.ppermute(value, AXES, pairs(target))


def after(value, *others):
    return lax.optimization_barrier((value, *others))[0]


def sibling(x, c, y, z, h):
    return x, 1 - c, y, z, h


def partner(x, c, y, z, h):
    return x, c, y, z, 1 - h


def along_x(step):
    return lambda x, c, y, z, h: (x + step, c, y, z, h)


NEAR = ((2, 0), (1, 0), (3, 0), (2, 1), (1, 1), (3, 1), (0, 1))
NEAR_Z = (4, 3, -3, 2, -2, 1, -1)


def near_target(i):
    def target(x, c, y, z, h):
        if c == 0:
            return x + NEAR[i][0], c, (y + NEAR[i][1]) % NY, z, h
        return x, c, y, z + NEAR_Z[i], h

    return target


def near_gather(own):
    first = [send(own, near_target(i)) for i in range(3)]
    own_later = after(own, *first)
    return [own] + first + [send(own_later, near_target(i)) for i in range(3, 7)]


def far_groups():
    groups = []
    for h in range(2):
        for x in range(NX):
            for y in range(NY):
                groups.append([device(x, 0, y, z, h) for z in range(NZ)])
        for z in range(NZ):
            groups.append([device(x, 1, y, z, h) for y in range(NY) for x in range(NX)])
    return groups


def place_kernel(at_ref, *refs):
    *blocks, out = refs
    for i, block in enumerate(blocks):
        rows = block.shape[0]
        start = pl.multiple_of(at_ref[i], 64)
        out[pl.ds(start, rows), :] = block[...]


def place(at, blocks):
    width = blocks[0].shape[1]
    total = sum(b.shape[0] for b in blocks)
    return pl.pallas_call(
        place_kernel,
        out_shape=jax.ShapeDtypeStruct((total, width), blocks[0].dtype),
        grid_spec=pltpu.PrefetchScalarGridSpec(
            num_scalar_prefetch=1,
            grid=(1,),
            in_specs=[pl.BlockSpec(b.shape, lambda i, at: (0, 0)) for b in blocks],
            out_specs=pl.BlockSpec((total, width), lambda i, at: (0, 0)),
        ),
        compiler_params=pltpu.CompilerParams(vmem_limit_bytes=VMEM_LIMIT),
        cost_estimate=pl.CostEstimate(
            flops=0, transcendentals=0, bytes_accessed=4 * total * width
        ),
        name="place",
    )(at, *blocks)


def norm_kernel(where_ref, own, other, gain, mine, theirs):
    first, second = own[...].astype(jnp.float32), other[...].astype(jnp.float32)
    square = jnp.sum(first * first + second * second, axis=-1, keepdims=True)
    scale = lax.rsqrt(square * (1.0 / D) + 1e-05)
    keep = where_ref[1] == 0
    halves = [
        (jnp.where(keep, a, b) * scale * gain[:, start : start + HALF]).astype(jnp.bfloat16)
        for a, b, start in ((first, second, 0), (second, first, HALF))
    ]

    def fill(by_z, by_plane):
        for z in range(NZ):
            for y in range(NY):
                start = z * 512 + y * 256
                by_z[:, start : start + 256] = halves[y][:, z * 256 : (z + 1) * 256]
        for y in range(NY):
            for x in range(NX):
                start = (y * NX + x) * 512
                starts = [z * 256 + x * 64 for z in range(NZ)]
                by_plane[:, start : start + 512] = jnp.concatenate(
                    [halves[y][:, at : at + 64] for at in starts], axis=1
                )

    @pl.when(where_ref[0] == 0)
    def _():
        fill(mine, theirs)

    @pl.when(where_ref[0] == 1)
    def _():
        fill(theirs, mine)


def normalize(where, own, other, gain):
    tile = 64
    shape = jax.ShapeDtypeStruct((SEQ, D), jnp.bfloat16)
    rows = pl.BlockSpec((tile, HALF), lambda i, w: (i, 0))
    out = pl.BlockSpec((tile, D), lambda i, w: (i, 0))
    return pl.pallas_call(
        norm_kernel,
        out_shape=(shape, shape),
        grid_spec=pltpu.PrefetchScalarGridSpec(
            num_scalar_prefetch=1,
            grid=(SEQ // tile,),
            in_specs=[rows, rows, pl.BlockSpec((1, D), lambda i, w: (0, 0))],
            out_specs=(out, out),
        ),
        compiler_params=pltpu.CompilerParams(vmem_limit_bytes=VMEM_LIMIT),
        cost_estimate=pl.CostEstimate(
            flops=8 * SEQ * D, transcendentals=0, bytes_accessed=6 * SEQ * D
        ),
        name="normalize",
    )(where, own, other, gain.reshape(1, D))


def project_kernel(rows, weights, out):
    out[...] = jnp.dot(rows[...], weights[...], preferred_element_type=jnp.float32)


def project(rows, weights):
    count, width = rows.shape[0], weights.shape[1]
    tile = 2 * HD
    return pl.pallas_call(
        project_kernel,
        out_shape=jax.ShapeDtypeStruct((count, width), jnp.float32),
        grid=(width // tile,),
        in_specs=[
            pl.BlockSpec((count, D), lambda n: (0, 0), pipeline_mode=pl.Buffered(1)),
            pl.BlockSpec((D, tile), lambda n: (0, n)),
        ],
        out_specs=pl.BlockSpec((count, tile), lambda n: (0, n)),
        compiler_params=pltpu.CompilerParams(vmem_limit_bytes=32 << 20),
        cost_estimate=pl.CostEstimate(
            flops=2 * count * D * width,
            transcendentals=0,
            bytes_accessed=2 * D * width + 2 * count * D + 4 * count * width,
        ),
        name="project",
    )(rows, weights)


def turn(values, cosine, sine):
    return values * cosine + pltpu.roll(values, HD // 2, 1) * sine


def attend_kernel(at_ref, q_ref, kv_ref, cos_ref, sin_ref, out, key, value):
    length = at_ref[0]
    cosine, sine = cos_ref[...], sin_ref[...]
    unit = D**-0.5
    tile = 256

    @pl.when(pl.program_id(0) == 0)
    def _():
        key[...] = turn(kv_ref[0, :, :HD] * unit, cosine, sine).astype(jnp.bfloat16)
        value[...] = (kv_ref[0, :, HD:] * unit).astype(jnp.bfloat16)

    s = lax.broadcasted_iota(jnp.int32, (tile, tile), 0)
    t = lax.broadcasted_iota(jnp.int32, (tile, tile), 1)
    heads = range(2)
    queries = [
        turn(q_ref[0, :, h * HD : (h + 1) * HD] * unit, cosine, sine).astype(jnp.bfloat16)
        for h in heads
    ]
    for block in range(SEQ // tile):
        start, reach = block * tile, (block + 1) * tile
        allowed = [jnp.where((t <= s) & (t + start < length), 0.0, -1e30)]
        if block:
            allowed.insert(0, jnp.where(t < length, 0.0, -1e30))
        live = lax.broadcasted_iota(jnp.int32, (tile, HD), 0) + start < length
        scores = lax.dot_general(
            jnp.concatenate([q[start:reach] for q in queries], axis=0),
            key[:reach],
            (((1,), (1,)), ((), ())),
            preferred_element_type=jnp.float32,
        )
        mask = jnp.concatenate(allowed, axis=1)
        scores = scores.reshape(len(heads), tile, reach) * (HD ** (-0.5) * LOG2E) + mask[None]
        scores = scores.reshape(len(heads) * tile, reach)
        raised = jnp.exp2(scores - jnp.max(scores, axis=1, keepdims=True))
        scale = 1.0 / jnp.sum(raised, axis=1, keepdims=True)
        mixed = jnp.dot(
            raised.astype(jnp.bfloat16), value[:reach], preferred_element_type=jnp.float32
        )
        mixed = mixed * scale
        for h in heads:
            out[start:reach, h * HD : (h + 1) * HD] = jnp.where(
                live, mixed[h * tile : (h + 1) * tile], 0.0
            ).astype(jnp.bfloat16)


def attend(length, row, proj, cosine, sine, columns, column):
    width = QPK * HD
    count = width // (2 * HD)
    at = jnp.stack([length, jnp.asarray(column // (2 * HD), jnp.int32)])
    return pl.pallas_call(
        attend_kernel,
        out_shape=jax.ShapeDtypeStruct((SEQ, columns), jnp.bfloat16),
        grid_spec=pltpu.PrefetchScalarGridSpec(
            num_scalar_prefetch=1,
            grid=(count,),
            in_specs=[
                pl.BlockSpec((1, SEQ, 2 * HD), lambda j, at: (row, 0, j)),
                pl.BlockSpec((1, SEQ, 2 * HD), lambda j, at: (row, 0, count)),
                pl.BlockSpec((SEQ, HD), lambda j, at: (0, 0)),
                pl.BlockSpec((SEQ, HD), lambda j, at: (0, 0)),
            ],
            out_specs=pl.BlockSpec((SEQ, 2 * HD), lambda j, at: (0, at[1] + j)),
            scratch_shapes=[
                pltpu.VMEM((SEQ, HD), jnp.bfloat16),
                pltpu.VMEM((SEQ, HD), jnp.bfloat16),
            ],
        ),
        compiler_params=pltpu.CompilerParams(vmem_limit_bytes=24 << 20),
        cost_estimate=pl.CostEstimate(
            flops=4 * SEQ * SEQ * width,
            transcendentals=SEQ * SEQ * width // HD,
            bytes_accessed=6 * SEQ * width,
        ),
        name="attend",
    )(at, proj, proj, cosine, sine)


def insert_kernel(at_ref, part, _, out):
    out[...] = part[...]


def insert(column, part, context):
    width = 4 * HD
    return pl.pallas_call(
        insert_kernel,
        out_shape=jax.ShapeDtypeStruct(context.shape, context.dtype),
        grid_spec=pltpu.PrefetchScalarGridSpec(
            num_scalar_prefetch=1,
            grid=(part.shape[1] // width,),
            in_specs=[
                pl.BlockSpec((SEQ, width), lambda j, at: (0, j)),
                pl.BlockSpec(memory_space=pl.ANY),
            ],
            out_specs=pl.BlockSpec((SEQ, width), lambda j, at: (0, at[0] + j)),
        ),
        input_output_aliases={2: 0},
        compiler_params=pltpu.CompilerParams(vmem_limit_bytes=VMEM_LIMIT),
        cost_estimate=pl.CostEstimate(
            flops=0, transcendentals=0, bytes_accessed=4 * SEQ * part.shape[1]
        ),
        name="insert",
    )(jnp.reshape(column // width, (1,)), part, context)


def per_device(pseudo_grads, counts, master, momentum, tokens, norm_gain, lengths):
    replica, fsdp = lax.axis_index("replica"), lax.axis_index("fsdp")
    x, core = replica // NC, replica % NC
    y, z = fsdp // NZ, fsdp % NZ
    cycle = jnp.where(y == 0, x, 7 - x)

    weight = counts[0].astype(jnp.float32)

    half = HD // 2
    freq = 500000.0 ** (-(jnp.arange(half, dtype=jnp.float32) * 2.0 / HD))
    angle = jnp.arange(SEQ, dtype=jnp.float32)[:, None] * freq[None, :]
    cosine, sine = jnp.cos(angle), jnp.sin(angle)
    cosine = jnp.concatenate([cosine, cosine], axis=1)
    sine = jnp.concatenate([-sine, sine], axis=1)

    def mine(array):
        return lax.dynamic_slice_in_dim(array, core * GROUP, GROUP, axis=1)

    def theirs(array):
        return lax.dynamic_slice_in_dim(array, (1 - core) * GROUP, GROUP, axis=1)

    grads = pseudo_grads[0]
    own_tokens = tokens[0]
    other_tokens = send(own_tokens, partner)


    counted = jnp.broadcast_to(weight, (8, GROUP))
    got = send(jnp.concatenate([theirs(grads) * weight, counted]), sibling)
    states = send(
        after(
            jnp.concatenate(
                [
                    theirs(master),
                    theirs(momentum),
                    jnp.broadcast_to(lengths[0].astype(jnp.float32), (8, GROUP)),
                ]
            ),
            got,
        ),
        sibling,
    )

    places_at = [jnp.where(core == 0, y * NX + x, z)]
    for (dx, dy), dz in zip(NEAR, NEAR_Z):
        plane = (y + NY - dy) % NY * NX + (x + NX - dx) % NX
        places_at.append(jnp.where(core == 0, plane, (z + NZ - dz) % NZ))
    places_at = (jnp.stack(places_at) * 64).astype(jnp.int32)

    summed = mine(grads) * weight + got[:256]
    part = summed.reshape(NX, 64, GROUP)

    def block(step):
        value = lax.dynamic_index_in_dim(part, (x + step) % NX, 0, keepdims=False)
        return jnp.concatenate([value, counted + got[256:]])

    arrived = [send(block(step), along_x(step)) for step in (1, 3, 2)]
    summed = block(0) + arrived[0] + arrived[1] + arrived[2]
    delta = summed[:64] / summed[64, 0]
    pair = []
    for array, kept in ((master, states[:32]), (momentum, states[32:64])):
        a, b = mine(array), kept
        pair.append(
            jnp.concatenate([jnp.where(core == 0, a, b), jnp.where(core == 0, b, a)], axis=0)
        )
    new_momentum = outer_momentum * pair[1] + delta
    new_master = pair[0] - outer_rate * (delta + outer_momentum * new_momentum)
    near = near_gather(new_master.astype(jnp.bfloat16))
    near[0] = after(near[0], other_tokens)
    whole = place(places_at, near)

    def in_order(own, other):
        return jnp.concatenate(
            [jnp.where(core == 0, own, other), jnp.where(core == 0, other, own)], axis=1
        )

    both = (new_master, new_momentum)
    back = send(
        after(
            jnp.concatenate([jnp.where(core == 0, v[32:], v[:32]) for v in both], axis=0),
            whole,
        ),
        sibling,
    )
    outs = [
        in_order(jnp.where(core == 0, v[:32], v[32:]), back[32 * i : 32 * (i + 1)])
        for i, v in enumerate(both)
    ]

    full = lax.all_gather(whole, AXES, axis=0, tiled=True, axis_index_groups=far_groups())
    where = jnp.stack([core, lax.axis_index("tensor")]).astype(jnp.int32)
    kept, given = normalize(where, own_tokens, after(other_tokens, whole), norm_gain)
    normed = jnp.concatenate([kept, send(given, sibling)])
    full = after(full, normed[-16:, -HD:], *outs)
    proj = project(normed, full).reshape(2, SEQ, GROUP)
    width = QPK * HD
    given = attend(states[64, 0].astype(jnp.int32), 1, proj, cosine, sine, width, 0)
    got = send(given, sibling)
    context = attend(lengths[0], 0, proj, cosine, sine, 2 * width, core * width)
    context = insert((1 - core) * width, got, context)
    return outs[0], outs[1], context[None]


def solution(mesh):
    in_specs = (
        P("replica", "fsdp", "tensor"),
        P("replica"),
        P(("fsdp", "replica"), "tensor"),
        P(("fsdp", "replica"), "tensor"),
        P(("replica", "fsdp"), None, "tensor"),
        P(),
        P(("replica", "fsdp")),
    )
    out_specs = (
        P(("fsdp", "replica"), "tensor"),
        P(("fsdp", "replica"), "tensor"),
        P(("replica", "fsdp"), None, "tensor"),
    )
    return jax.shard_map(
        per_device, mesh=mesh, in_specs=in_specs, out_specs=out_specs, check_vma=False
    )
```

```python
import jax
import jax.numpy as jnp
from jax import lax
from jax.experimental import pallas as pl
from jax.experimental.pallas import tpu as pltpu
from jax.sharding import PartitionSpec as P

D = 4096
HD = 128
QPK = 8
SEQ = 512
GROUP = (QPK + 2) * HD
HALF = D // 2
VMEM_LIMIT = 60 << 20
LOG2E = 1.4426950408889634
AXES = ("replica", "fsdp", "tensor")
NX, NC, NY, NZ = 4, 2, 2, 8

outer_momentum = 0.9
outer_rate = 0.7


def device(x, c, y, z, h):
    return (((x % NX) * NC + c) * NY * NZ + y * NZ + z % NZ) * 2 + h


def places():
    for x in range(NX):
        for c in range(NC):
            for y in range(NY):
                for z in range(NZ):
                    for h in range(2):
                        yield x, c, y, z, h


def pairs(target):
    return [(device(*p), device(*target(*p))) for p in places()]


def send(value, target):
    return lax.ppermute(value, AXES, pairs(target))


def after(value, *others):
    return lax.optimization_barrier((value, *others))[0]


def sibling(x, c, y, z, h):
    return x, 1 - c, y, z, h


def partner(x, c, y, z, h):
    return x, c, y, z, 1 - h


def along_x(step):
    return lambda x, c, y, z, h: (x + step, c, y, z, h)


NEAR = ((2, 0), (1, 0), (3, 0), (2, 1), (1, 1), (3, 1), (0, 1))
NEAR_Z = (4, 3, -3, 2, -2, 1, -1)


def near_target(i):
    def target(x, c, y, z, h):
        if c == 0:
            return x + NEAR[i][0], c, (y + NEAR[i][1]) % NY, z, h
        return x, c, y, z + NEAR_Z[i], h

    return target


def near_gather(own):
    first = [send(own, near_target(i)) for i in range(3)]
    own_later = after(own, *first)
    return [own] + first + [send(own_later, near_target(i)) for i in range(3, 7)]


def far_groups():
    groups = []
    for h in range(2):
        for x in range(NX):
            for y in range(NY):
                groups.append([device(x, 0, y, z, h) for z in range(NZ)])
        for z in range(NZ):
            groups.append([device(x, 1, y, z, h) for y in range(NY) for x in range(NX)])
    return groups


def place_kernel(at_ref, *refs):
    *blocks, out = refs
    for i, block in enumerate(blocks):
        rows = block.shape[0]
        start = pl.multiple_of(at_ref[i], 64)
        out[pl.ds(start, rows), :] = block[...]


def place(at, blocks):
    width = blocks[0].shape[1]
    total = sum(b.shape[0] for b in blocks)
    return pl.pallas_call(
        place_kernel,
        out_shape=jax.ShapeDtypeStruct((total, width), blocks[0].dtype),
        grid_spec=pltpu.PrefetchScalarGridSpec(
            num_scalar_prefetch=1,
            grid=(1,),
            in_specs=[pl.BlockSpec(b.shape, lambda i, at: (0, 0)) for b in blocks],
            out_specs=pl.BlockSpec((total, width), lambda i, at: (0, 0)),
        ),
        compiler_params=pltpu.CompilerParams(vmem_limit_bytes=VMEM_LIMIT),
        cost_estimate=pl.CostEstimate(
            flops=0, transcendentals=0, bytes_accessed=4 * total * width
        ),
        name="place",
    )(at, *blocks)


def norm_kernel(where_ref, own, other, gain, mine, theirs):
    first, second = own[...].astype(jnp.float32), other[...].astype(jnp.float32)
    square = jnp.sum(first * first + second * second, axis=-1, keepdims=True)
    scale = lax.rsqrt(square * (1.0 / D) + 1e-05)
    keep = where_ref[1] == 0
    halves = [
        (jnp.where(keep, a, b) * scale * gain[:, start : start + HALF]).astype(jnp.bfloat16)
        for a, b, start in ((first, second, 0), (second, first, HALF))
    ]

    def fill(by_z, by_plane):
        for z in range(NZ):
            for y in range(NY):
                start = z * 512 + y * 256
                by_z[:, start : start + 256] = halves[y][:, z * 256 : (z + 1) * 256]
        for y in range(NY):
            for x in range(NX):
                start = (y * NX + x) * 512
                starts = [z * 256 + x * 64 for z in range(NZ)]
                by_plane[:, start : start + 512] = jnp.concatenate(
                    [halves[y][:, at : at + 64] for at in starts], axis=1
                )

    @pl.when(where_ref[0] == 0)
    def _():
        fill(mine, theirs)

    @pl.when(where_ref[0] == 1)
    def _():
        fill(theirs, mine)


def normalize(where, own, other, gain):
    tile = 64
    shape = jax.ShapeDtypeStruct((SEQ, D), jnp.bfloat16)
    rows = pl.BlockSpec((tile, HALF), lambda i, w: (i, 0))
    out = pl.BlockSpec((tile, D), lambda i, w: (i, 0))
    return pl.pallas_call(
        norm_kernel,
        out_shape=(shape, shape),
        grid_spec=pltpu.PrefetchScalarGridSpec(
            num_scalar_prefetch=1,
            grid=(SEQ // tile,),
            in_specs=[rows, rows, pl.BlockSpec((1, D), lambda i, w: (0, 0))],
            out_specs=(out, out),
        ),
        compiler_params=pltpu.CompilerParams(vmem_limit_bytes=VMEM_LIMIT),
        cost_estimate=pl.CostEstimate(
            flops=8 * SEQ * D, transcendentals=0, bytes_accessed=6 * SEQ * D
        ),
        name="normalize",
    )(where, own, other, gain.reshape(1, D))


def project_kernel(rows, weights, out):
    out[...] = jnp.dot(rows[...], weights[...], preferred_element_type=jnp.float32)


def project(rows, weights):
    count, width = rows.shape[0], weights.shape[1]
    tile = 2 * HD
    return pl.pallas_call(
        project_kernel,
        out_shape=jax.ShapeDtypeStruct((count, width), jnp.float32),
        grid=(width // tile,),
        in_specs=[
            pl.BlockSpec((count, D), lambda n: (0, 0), pipeline_mode=pl.Buffered(1)),
            pl.BlockSpec((D, tile), lambda n: (0, n)),
        ],
        out_specs=pl.BlockSpec((count, tile), lambda n: (0, n)),
        compiler_params=pltpu.CompilerParams(vmem_limit_bytes=24 << 20),
        cost_estimate=pl.CostEstimate(
            flops=2 * count * D * width,
            transcendentals=0,
            bytes_accessed=2 * D * width + 2 * count * D + 4 * count * width,
        ),
        name="project",
    )(rows, weights)


def turn(values, cosine, sine):
    return values * cosine + pltpu.roll(values, HD // 2, 1) * sine


def attend_kernel(at_ref, q_ref, kv_ref, cos_ref, sin_ref, out, key, value):
    length = at_ref[0]
    cosine, sine = cos_ref[...], sin_ref[...]
    unit = D**-0.5
    tile = 256

    @pl.when(pl.program_id(0) == 0)
    def _():
        key[...] = turn(kv_ref[0, :, :HD] * unit, cosine, sine).astype(jnp.bfloat16)
        value[...] = (kv_ref[0, :, HD:] * unit).astype(jnp.bfloat16)

    s = lax.broadcasted_iota(jnp.int32, (tile, tile), 0)
    t = lax.broadcasted_iota(jnp.int32, (tile, tile), 1)
    heads = range(2)
    queries = [
        turn(q_ref[0, :, h * HD : (h + 1) * HD] * unit, cosine, sine).astype(jnp.bfloat16)
        for h in heads
    ]
    for block in range(SEQ // tile):
        start, reach = block * tile, (block + 1) * tile
        allowed = [jnp.where((t <= s) & (t + start < length), 0.0, -1e30)]
        if block:
            allowed.insert(0, jnp.where(t < length, 0.0, -1e30))
        live = lax.broadcasted_iota(jnp.int32, (tile, HD), 0) + start < length
        scores = lax.dot_general(
            jnp.concatenate([q[start:reach] for q in queries], axis=0),
            key[:reach],
            (((1,), (1,)), ((), ())),
            preferred_element_type=jnp.float32,
        )
        mask = jnp.concatenate(allowed, axis=1)
        scores = scores.reshape(len(heads), tile, reach) * (HD ** (-0.5) * LOG2E) + mask[None]
        scores = scores.reshape(len(heads) * tile, reach)
        raised = jnp.exp2(scores - jnp.max(scores, axis=1, keepdims=True))
        scale = 1.0 / jnp.sum(raised, axis=1, keepdims=True)
        mixed = jnp.dot(
            raised.astype(jnp.bfloat16), value[:reach], preferred_element_type=jnp.float32
        )
        mixed = mixed * scale
        for h in heads:
            out[start:reach, h * HD : (h + 1) * HD] = jnp.where(
                live, mixed[h * tile : (h + 1) * tile], 0.0
            ).astype(jnp.bfloat16)


def attend(length, row, proj, cosine, sine, columns, column):
    width = QPK * HD
    count = width // (2 * HD)
    at = jnp.stack([length, jnp.asarray(column // (2 * HD), jnp.int32)])
    return pl.pallas_call(
        attend_kernel,
        out_shape=jax.ShapeDtypeStruct((SEQ, columns), jnp.bfloat16),
        grid_spec=pltpu.PrefetchScalarGridSpec(
            num_scalar_prefetch=1,
            grid=(count,),
            in_specs=[
                pl.BlockSpec((1, SEQ, 2 * HD), lambda j, at: (row, 0, j)),
                pl.BlockSpec((1, SEQ, 2 * HD), lambda j, at: (row, 0, count)),
                pl.BlockSpec((SEQ, HD), lambda j, at: (0, 0)),
                pl.BlockSpec((SEQ, HD), lambda j, at: (0, 0)),
            ],
            out_specs=pl.BlockSpec((SEQ, 2 * HD), lambda j, at: (0, at[1] + j)),
            scratch_shapes=[
                pltpu.VMEM((SEQ, HD), jnp.bfloat16),
                pltpu.VMEM((SEQ, HD), jnp.bfloat16),
            ],
        ),
        compiler_params=pltpu.CompilerParams(vmem_limit_bytes=16 << 20),
        cost_estimate=pl.CostEstimate(
            flops=4 * SEQ * SEQ * width,
            transcendentals=SEQ * SEQ * width // HD,
            bytes_accessed=6 * SEQ * width,
        ),
        name="attend",
    )(at, proj, proj, cosine, sine)


def insert_kernel(at_ref, part, _, out):
    out[...] = part[...]


def insert(column, part, context):
    width = 4 * HD
    return pl.pallas_call(
        insert_kernel,
        out_shape=jax.ShapeDtypeStruct(context.shape, context.dtype),
        grid_spec=pltpu.PrefetchScalarGridSpec(
            num_scalar_prefetch=1,
            grid=(part.shape[1] // width,),
            in_specs=[
                pl.BlockSpec((SEQ, width), lambda j, at: (0, j)),
                pl.BlockSpec(memory_space=pl.ANY),
            ],
            out_specs=pl.BlockSpec((SEQ, width), lambda j, at: (0, at[0] + j)),
        ),
        input_output_aliases={2: 0},
        compiler_params=pltpu.CompilerParams(vmem_limit_bytes=16 << 20),
        cost_estimate=pl.CostEstimate(
            flops=0, transcendentals=0, bytes_accessed=4 * SEQ * part.shape[1]
        ),
        name="insert",
    )(jnp.reshape(column // width, (1,)), part, context)


def per_device(pseudo_grads, counts, master, momentum, tokens, norm_gain, lengths):
    replica, fsdp = lax.axis_index("replica"), lax.axis_index("fsdp")
    x, core = replica // NC, replica % NC
    y, z = fsdp // NZ, fsdp % NZ
    cycle = jnp.where(y == 0, x, 7 - x)

    weight = counts[0].astype(jnp.float32)

    half = HD // 2
    freq = 500000.0 ** (-(jnp.arange(half, dtype=jnp.float32) * 2.0 / HD))
    angle = jnp.arange(SEQ, dtype=jnp.float32)[:, None] * freq[None, :]
    cosine, sine = jnp.cos(angle), jnp.sin(angle)
    cosine = jnp.concatenate([cosine, cosine], axis=1)
    sine = jnp.concatenate([-sine, sine], axis=1)

    def mine(array):
        return lax.dynamic_slice_in_dim(array, core * GROUP, GROUP, axis=1)

    def theirs(array):
        return lax.dynamic_slice_in_dim(array, (1 - core) * GROUP, GROUP, axis=1)

    grads = pseudo_grads[0]
    own_tokens = tokens[0]
    other_tokens = send(own_tokens, partner)


    counted = jnp.broadcast_to(weight, (8, GROUP))
    got = send(jnp.concatenate([theirs(grads) * weight, counted]), sibling)
    states = send(
        after(
            jnp.concatenate(
                [
                    theirs(master),
                    theirs(momentum),
                    jnp.broadcast_to(lengths[0].astype(jnp.float32), (8, GROUP)),
                ]
            ),
            got,
        ),
        sibling,
    )

    places_at = [jnp.where(core == 0, y * NX + x, z)]
    for (dx, dy), dz in zip(NEAR, NEAR_Z):
        plane = (y + NY - dy) % NY * NX + (x + NX - dx) % NX
        places_at.append(jnp.where(core == 0, plane, (z + NZ - dz) % NZ))
    places_at = (jnp.stack(places_at) * 64).astype(jnp.int32)

    summed = mine(grads) * weight + got[:256]
    part = summed.reshape(NX, 64, GROUP)

    def block(step):
        value = lax.dynamic_index_in_dim(part, (x + step) % NX, 0, keepdims=False)
        return jnp.concatenate([value, counted + got[256:]])

    arrived = [send(block(step), along_x(step)) for step in (1, 3, 2)]
    summed = block(0) + arrived[0] + arrived[1] + arrived[2]
    delta = summed[:64] / summed[64, 0]
    pair = []
    for array, kept in ((master, states[:32]), (momentum, states[32:64])):
        a, b = mine(array), kept
        pair.append(
            jnp.concatenate([jnp.where(core == 0, a, b), jnp.where(core == 0, b, a)], axis=0)
        )
    new_momentum = outer_momentum * pair[1] + delta
    new_master = pair[0] - outer_rate * (delta + outer_momentum * new_momentum)
    near = near_gather(new_master.astype(jnp.bfloat16))
    near[0] = after(near[0], other_tokens)
    whole = place(places_at, near)

    def in_order(own, other):
        return jnp.concatenate(
            [jnp.where(core == 0, own, other), jnp.where(core == 0, other, own)], axis=1
        )

    both = (new_master, new_momentum)
    back = send(
        after(
            jnp.concatenate([jnp.where(core == 0, v[32:], v[:32]) for v in both], axis=0),
            whole,
        ),
        sibling,
    )
    outs = [
        in_order(jnp.where(core == 0, v[:32], v[32:]), back[32 * i : 32 * (i + 1)])
        for i, v in enumerate(both)
    ]

    full = lax.all_gather(whole, AXES, axis=0, tiled=True, axis_index_groups=far_groups())
    where = jnp.stack([core, lax.axis_index("tensor")]).astype(jnp.int32)
    kept, given = normalize(where, own_tokens, after(other_tokens, whole), norm_gain)
    normed = jnp.concatenate([kept, send(given, sibling)])
    full = after(full, normed[-16:, -HD:], *outs)
    proj = project(normed, full).reshape(2, SEQ, GROUP)
    width = QPK * HD
    given = attend(states[64, 0].astype(jnp.int32), 1, proj, cosine, sine, width, 0)
    got = send(given, sibling)
    context = attend(lengths[0], 0, proj, cosine, sine, 2 * width, core * width)
    context = insert((1 - core) * width, got, context)
    return outs[0], outs[1], context[None]


def solution(mesh):
    in_specs = (
        P("replica", "fsdp", "tensor"),
        P("replica"),
        P(("fsdp", "replica"), "tensor"),
        P(("fsdp", "replica"), "tensor"),
        P(("replica", "fsdp"), None, "tensor"),
        P(),
        P(("replica", "fsdp")),
    )
    out_specs = (
        P(("fsdp", "replica"), "tensor"),
        P(("fsdp", "replica"), "tensor"),
        P(("replica", "fsdp"), None, "tensor"),
    )
    return jax.shard_map(
        per_device, mesh=mesh, in_specs=in_specs, out_specs=out_specs, check_vma=False
    )
```
